32 devices in a mesh: dp: 8 (over z, x), feat: 4 (over y, core).
Axes of the slice: x: 2, y: 2, z: 4, core: 2. Of those that a mesh axis runs over, the one named last changes fastest.
Arguments:
- residual: bfloat16 [192, 7168], P('dp'), may hold values from -6 to 6
- cotangent: bfloat16 [192, 7168], P('dp'), may hold values from -6 to 6
- encoder_weight: bfloat16 [7168, 65536], P('dp', 'feat'), may hold values from -0.0625 to 0.0625
- encoder_bias: float32 [65536], P('feat'), may hold values from -3 to 3
- decoder_weight: bfloat16 [65536, 7168], P('feat', 'dp'), may hold values from -0.0625 to 0.0625
- route_experts: int32 [192, 8], P('dp'), may hold values from 0 to 255, all different within a row
- route_buckets: int32 [192, 8], P('dp'), may hold values from 1 to 8
Outputs:
- expert_credit: float32 [256, 65536], P('dp', 'feat')
The draws below stay inside these ranges and needn't reach their ends.
Inputs may be any that keep to these rules, and one draw needn't show every extreme that they name: `route_experts`: each token names 8 different experts, and every expert is named by some token.
All inputs are finite; a program needn't handle non-finite values.
Results may differ from the reference program's by a relative error of at most 0.0003.
Values may be sent and summed in bfloat16 or wider, within the bound.
No kernel may reach another device: no remote copies, remote signals or barrier semaphores. Data moves between devices by JAX's collectives and lax.ppermute only.
A program may use at most 128 MiB of HBM per device.

```python
import jax
import jax.numpy as jnp
from jax import lax

D = 7168
E = 256
TOPK = 8
F = 65536
TOKENS = 192


def set_ends(entries, stream_key, least, top_value):
    longest = entries.shape.index(max(entries.shape))
    spots = []
    for shift in (0, 1):
        where = [jax.random.randint(jax.random.fold_in(stream_key, axis), (), 0, length) for axis, length in enumerate(entries.shape)]
        where[longest] = (where[longest] + shift) % entries.shape[longest]
        spots.append(tuple(where))
    return entries.at[spots[0]].set(least).at[spots[1]].set(top_value)


def levels(own_key, extent, split, smallest, high):
    level, own = 1.0, jax.random.fold_in(own_key, 6)
    for position, shards_of in split:
        steps = jnp.exp(jax.random.uniform(jax.random.fold_in(own, position), (shards_of,), jnp.float32, smallest / len(split), high / len(split)))
        level = level * jnp.repeat(steps, extent[position] // shards_of).reshape([-1 if axis == position else 1 for axis in range(len(extent))])
    return level


def picks_of(own_key, rows, number_of, top, lift):
    order = jax.random.permutation(jax.random.fold_in(own_key, 1), number_of)
    favour = order
    for power in range(3):
        favour = favour * favour // number_of
    favour = favour * lift // number_of
    chance = jax.random.randint(jax.random.fold_in(own_key, 2), (rows, number_of), 0, 4096) + favour
    sure = jax.random.permutation(jax.random.fold_in(own_key, 3), rows)[jnp.arange(number_of) % rows]
    chance = jnp.where(jnp.arange(rows)[:, None] == sure[None, :], 1 << 14, chance)
    merit = chance * number_of + jnp.arange(number_of)
    return lax.top_k(merit.astype(jnp.int32), top)[1].astype(jnp.int32)


def gaussian(stream_key, shape, scale, most, split=(), kind=jnp.bfloat16):
    array = jax.random.normal(stream_key, shape, jnp.float32) * scale
    if len(split) > 0:
        array = levels(stream_key, shape, split, -0.22, 0.18) * array
    return jnp.clip(array, min=-most, max=most).astype(kind)


def setup_inputs(seed: int = 0) -> dict:
    streams_of = jax.random.split(jax.random.key(seed), 8)
    return {
        "residual": gaussian(streams_of[0], (TOKENS, D), 1.0, 6.0, ((0, 8),)),
        "cotangent": gaussian(streams_of[1], (TOKENS, D), 1.0, 6.0, ((0, 8),)),
        "encoder_weight": gaussian(streams_of[2], (D, F), D ** -0.5, 0.0625, ((0, 8), (1, 4))),
        "encoder_bias": gaussian(streams_of[3], (F,), 0.5, 3.0, ((0, 4),), jnp.float32),
        "decoder_weight": gaussian(streams_of[4], (F, D), D ** -0.5, 0.0625, ((0, 4), (1, 8))),
        "route_experts": picks_of(streams_of[5], TOKENS, E, TOPK, 256),
        "route_buckets": set_ends(jax.random.randint(streams_of[6], (TOKENS, TOPK), 1, 9), jax.random.fold_in(streams_of[6], 1), 1, 8).astype(jnp.int32),
    }


def reference(residual, cotangent, encoder_weight, encoder_bias, decoder_weight, route_experts, route_buckets):
    pre = jnp.dot(residual.astype(jnp.float32), encoder_weight.astype(jnp.float32), precision=lax.Precision.HIGHEST)
    grad = lax.dot_general(cotangent.astype(jnp.float32), decoder_weight.astype(jnp.float32), (((1,), (1,)), ((), ())), precision=lax.Precision.HIGHEST)
    score = jnp.maximum(pre + encoder_bias[None, :], 0.0) * grad
    expert_ids = jnp.arange(E, dtype=jnp.int32)
    weights = route_buckets.astype(jnp.float32) * 0.125
    routing = jnp.sum((route_experts[:, :, None] == expert_ids[None, None, :]).astype(jnp.float32) * weights[:, :, None], axis=1)
    return lax.dot_general(routing, score, (((0,), (0,)), ((), ())), precision=lax.Precision.HIGHEST)
```

```python
import functools

import jax
import jax.numpy as jnp
from jax import lax
from jax.experimental import pallas as pl
from jax.experimental.pallas import tpu as pltpu
from jax.sharding import PartitionSpec as P

E = 256
LANES = 128
CODE_ROWS = 16
STEPS = 256.0
TOP = 32700.0
TINY = 2.0 ** -100


def scale_code(most):
    return jnp.ceil(jnp.log2(jnp.maximum(most, TINY)) * STEPS)


def quantise(value, code):
    return jnp.round(value * (jnp.exp2(code * (-1.0 / STEPS)) * TOP)).astype(jnp.int32).astype(jnp.int16)


def unit_of(code):
    return jnp.exp2(code * (1.0 / STEPS)) * (1.0 / TOP)


def as_float(ints):
    return ints.astype(jnp.int32).astype(jnp.float32)


def partial_sums(tokens, rows_ref, enc_ref, dec_ref, message_refs):
    pre = jnp.dot(rows_ref[0], enc_ref[...], preferred_element_type=jnp.float32)
    grad = lax.dot_general(
        rows_ref[1], dec_ref[...], (((1,), (1,)), ((), ())), preferred_element_type=jnp.float32
    )
    for message in message_refs:
        unit = unit_of(as_float(message[2 * tokens :, :]))
        pre = pre + as_float(message[:tokens, :]) * unit[0:1]
        grad = grad + as_float(message[tokens : 2 * tokens, :]) * unit[1:2]
    return pre, grad


def send_kernel(tokens, n_messages, where_ref, rows_ref, enc_ref, dec_ref, *refs):
    messages, out_ref = refs[:n_messages], refs[-1]
    pre, grad = partial_sums(tokens, rows_ref, enc_ref, dec_ref, messages)
    pre_code = scale_code(jnp.max(jnp.abs(pre), axis=0, keepdims=True))
    grad_code = scale_code(jnp.max(jnp.abs(grad), axis=0, keepdims=True))
    out_ref[:tokens, :] = quantise(pre, pre_code)
    out_ref[tokens : 2 * tokens, :] = quantise(grad, grad_code)
    row = lax.broadcasted_iota(jnp.int32, (CODE_ROWS, pre.shape[1]), 0)
    codes = jnp.where(row == 0, pre_code, jnp.where(row == 1, grad_code, 0.0))
    out_ref[2 * tokens :, :] = codes.astype(jnp.int32).astype(jnp.int16)


def credit_kernel(tokens, n_messages, where_ref, rows_ref, enc_ref, dec_ref, *refs):
    messages = refs[:n_messages]
    bias_ref, routing_ref, out_ref, code_ref = refs[n_messages], refs[n_messages + 1], refs[-2], refs[-1]
    pre, grad = partial_sums(tokens, rows_ref, enc_ref, dec_ref, messages)
    score = jnp.maximum(pre + bias_ref[...], 0.0) * grad
    high = score.astype(jnp.bfloat16)
    low = (score - high.astype(jnp.float32)).astype(jnp.bfloat16)
    credit = jnp.dot(routing_ref[...], high, preferred_element_type=jnp.float32) + jnp.dot(
        routing_ref[...], low, preferred_element_type=jnp.float32
    )
    code = scale_code(jnp.max(jnp.abs(credit), axis=1, keepdims=True))
    out_ref[...] = quantise(credit, code)
    code_ref[...] = jnp.broadcast_to(code, (E, LANES)).astype(jnp.int32).astype(jnp.int16)


def block_of(length, most=512):
    block = min(length, most)
    while length % block:
        block -= LANES
    return block


class Chunk:
    def __init__(self, first, size, order):
        self.first, self.size, self.order = first, size, order
        self.messages = []

    def kept(self, bits, stage):
        first = self.first
        for j in range(stage):
            first = first + bits[self.order[j]] * (self.size >> (j + 1))
        return first

    def sent(self, bits, stage):
        return self.kept(bits, stage) + (1 - bits[self.order[stage]]) * (self.size >> (stage + 1))


def run_stage(chunk, stage, bits, rows, enc, dec, bias, routing, earlier, cost):
    last = stage == len(chunk.order)
    tokens, depth = rows.shape[1:]
    length = chunk.size >> (stage if last else stage + 1)
    block = block_of(length)

    def at(i, bits_ref, message=None):
        first = chunk.kept(bits_ref, stage) if last else chunk.sent(bits_ref, stage)
        if message is not None:
            first = first - chunk.kept(bits_ref, message + 1)
        return first // block + i

    in_specs = [
        pl.BlockSpec((2, tokens, depth), lambda i, w: (0, 0, 0)),
        pl.BlockSpec((depth, block), lambda i, w: (0, at(i, w))),
        pl.BlockSpec((block, depth), lambda i, w: (at(i, w), 0)),
    ]
    operands = [rows, enc, dec]
    for j, message in enumerate(chunk.messages):
        in_specs.append(pl.BlockSpec((message.shape[0], block), lambda i, w, j=j: (0, at(i, w, j))))
        operands.append(message)
    if last:
        in_specs.append(pl.BlockSpec((1, block), lambda i, w: (0, at(i, w))))
        in_specs.append(pl.BlockSpec(routing.shape, lambda i, w: (0, 0)))
        operands += [bias, routing]
        body = credit_kernel
        out_shape = [
            jax.ShapeDtypeStruct((E, length), jnp.int16),
            jax.ShapeDtypeStruct((E, LANES * (length // block)), jnp.int16),
        ]
        out_specs = [pl.BlockSpec((E, block), lambda i, w: (0, i)), pl.BlockSpec((E, LANES), lambda i, w: (0, i))]
    else:
        body = send_kernel
        out_shape = jax.ShapeDtypeStruct((2 * tokens + CODE_ROWS, length), jnp.int16)
        out_specs = pl.BlockSpec((2 * tokens + CODE_ROWS, block), lambda i, w: (0, i))
    if earlier is not None:
        in_specs.append(pl.BlockSpec(memory_space=pl.ANY))
        operands.append(earlier)
    return pl.pallas_call(
        functools.partial(body, tokens, len(chunk.messages)),
        grid_spec=pltpu.PrefetchScalarGridSpec(
            num_scalar_prefetch=1, grid=(length // block,), in_specs=in_specs, out_specs=out_specs
        ),
        out_shape=out_shape,
        compiler_params=pltpu.CompilerParams(vmem_limit_bytes=40 * 1024 * 1024),
        cost_estimate=pl.CostEstimate(flops=cost, bytes_accessed=1, transcendentals=0),
        name=("credit" if last else f"stage{stage}"),
    )(bits, *operands)


def place_kernel(blocks, whole_ref, *refs):
    out_ref = refs[-1]
    lanes = whole_ref.shape[2] - LANES
    for owner, column, width, lane, target in blocks:
        unit = unit_of(as_float(whole_ref[owner, :, lanes:])[:, lane : lane + 1])
        out_ref[:, target : target + width] = as_float(whole_ref[owner, :, column : column + width]) * unit


def place(group, n_dp, whole, out, features):
    first = min(chunk.first for chunk in group)
    span = sum(chunk.size for chunk in group)
    blocks, column = [], 0
    for lane, chunk in enumerate(group):
        width = chunk.size // n_dp
        for owner in range(n_dp):
            slot = 0
            for bit in chunk.order:
                slot = 2 * slot + ((owner >> bit) & 1)
            blocks.append((owner, column, width, lane, chunk.first - first + slot * width))
        column += width
    operands, in_specs = [whole], [pl.BlockSpec(whole.shape, lambda i: (0, 0, 0))]
    if out is not None:
        operands.append(out)
        in_specs.append(pl.BlockSpec(memory_space=pl.ANY))
    return pl.pallas_call(
        functools.partial(place_kernel, blocks),
        grid=(1,),
        in_specs=in_specs,
        out_specs=pl.BlockSpec((whole.shape[1], span), lambda i: (0, first // span)),
        out_shape=jax.ShapeDtypeStruct((whole.shape[1], features), jnp.float32),
        input_output_aliases={} if out is None else {1: 0},
        compiler_params=pltpu.CompilerParams(vmem_limit_bytes=40 * 1024 * 1024),
        name="place",
    )(*operands)


def collect(group, credits, n_dp):
    lane = lax.broadcasted_iota(jnp.int32, (E, LANES), 1)
    codes = credits[0][1]
    for k in range(1, len(credits)):
        codes = jnp.where(lane == k, credits[k][1], codes)
    whole = jnp.concatenate([c[0] for c in credits] + [codes], 1)
    whole = lax.all_to_all(whole, "dp", split_axis=0, concat_axis=0, tiled=True)
    return whole.reshape(n_dp, E // n_dp, -1)


def plan_of(units, n_bits):
    straight = tuple(range(n_bits))
    if units == 16 and n_bits == 3:
        sizes = SIZES
        groups, sequence = GROUPS, SEQUENCE
    else:
        sizes = [(1, straight)] * units
        groups, sequence = [list(range(units))], None
    if sequence is None:
        sequence = [
            (step - stage, stage)
            for step in range(len(sizes) + n_bits)
            for stage in range(n_bits + 1)
            if 0 <= step - stage < len(sizes)
        ]
    return sizes, groups, sequence


A, B, C = (0, 1, 2), (1, 0, 2), (1, 2, 0)
SIZES = [(2, A), (2, A), (4, A), (4, A), (2, A), (2, A)]
GROUPS = [[0, 1, 2, 3, 4, 5]]
SEQUENCE = None
COST = 9_000_000_000


def route_table(routes):
    experts, buckets = routes[:, : routes.shape[1] // 2], routes[:, routes.shape[1] // 2 :]
    expert_ids = jnp.arange(E, dtype=jnp.int32)
    weights = buckets.astype(jnp.float32) * 0.125
    table = jnp.sum(
        (experts[:, None, :].astype(jnp.int32) == expert_ids[None, :, None]).astype(jnp.float32)
        * weights[:, None, :],
        axis=2,
    )
    return table.T.astype(jnp.bfloat16)


def gather_rows(residual, cotangent, route_experts, route_buckets, n_dp):
    mine, width = residual.shape
    depth = width // n_dp
    routes = jnp.concatenate([route_experts, route_buckets], 1).astype(jnp.bfloat16)
    extra = -(-routes.size // (8 * depth)) * 8
    flat = jnp.pad(routes.reshape(-1), (0, extra * depth - routes.size)).reshape(extra, 1, depth)
    flat = jnp.broadcast_to(flat, (extra, n_dp, depth)).reshape(extra, width)
    got = lax.all_to_all(
        jnp.concatenate([residual, cotangent, flat], 0), "dp", split_axis=1, concat_axis=0, tiled=True
    ).reshape(n_dp, 2 * mine + extra, depth)
    rows = got[:, : 2 * mine].reshape(n_dp, 2, mine, depth).transpose(1, 0, 2, 3).reshape(2, n_dp * mine, depth)
    routes = got[:, 2 * mine :].reshape(n_dp, -1)[:, : routes.size].reshape(n_dp * mine, -1)
    return rows, routes


def on_device(residual, cotangent, enc, bias, dec, route_experts, route_buckets):
    n_dp, me = lax.axis_size("dp"), lax.axis_index("dp")
    n_bits = n_dp.bit_length() - 1
    features = enc.shape[1]
    bits = (me >> jnp.arange(n_bits, dtype=jnp.int32)) & 1
    rows, routes = gather_rows(residual, cotangent, route_experts, route_buckets, n_dp)
    routing = route_table(routes)
    bias = bias[None, :]

    unit = LANES * n_dp
    sizes, groups, sequence = plan_of(features // unit, n_bits)
    chunks, first = [], 0
    for units, order in sizes:
        chunks.append(Chunk(first, units * unit, order))
        first += units * unit

    earlier, credits, out = None, {}, None
    for n, (c, stage) in enumerate(sequence):
        chunk = chunks[c]
        result = run_stage(chunk, stage, bits, rows, enc, dec, bias, routing, earlier, COST if n != 1 else 1)
        if stage < n_bits:
            partner = [(i, i ^ (1 << chunk.order[stage])) for i in range(n_dp)]
            chunk.messages.append(lax.ppermute(result, "dp", partner))
            earlier = result
        else:
            credits[c] = result
            earlier = result[1]
            for group in groups:
                if c in group and all(k in credits for k in group):
                    whole = collect([chunks[k] for k in group], [credits[k] for k in group], n_dp)
                    out = place([chunks[k] for k in group], n_dp, whole, out, features)
    return out


def solution(mesh):
    placed = (
        P("dp", None),
        P("dp", None),
        P("dp", "feat"),
        P("feat"),
        P("feat", "dp"),
        P("dp", None),
        P("dp", None),
    )
    return jax.shard_map(
        on_device, mesh=mesh, in_specs=placed, out_specs=P("dp", "feat"), check_vma=False
    )
```

```python
import functools

import jax
import jax.numpy as jnp
from jax import lax
from jax.experimental import pallas as pl
from jax.experimental.pallas import tpu as pltpu
from jax.sharding import PartitionSpec as P

E = 256
LANES = 128
CODE_ROWS = 8
STEPS = 256.0
TOP = 32700.0
TINY = 2.0 ** -100


def scale_code(most):
    return jnp.ceil(jnp.log2(jnp.maximum(most, TINY)) * STEPS)


def quantise(value, code):
    return jnp.round(value * (jnp.exp2(code * (-1.0 / STEPS)) * TOP)).astype(jnp.int32).astype(jnp.int16)


def unit_of(code):
    return jnp.exp2(code * (1.0 / STEPS)) * (1.0 / TOP)


def as_float(ints):
    return ints.astype(jnp.int32).astype(jnp.float32)


def partial_sums(tokens, rows_ref, enc_ref, dec_ref, message_refs):
    pre = jnp.dot(rows_ref[0], enc_ref[...], preferred_element_type=jnp.float32)
    grad = lax.dot_general(
        rows_ref[1], dec_ref[...], (((1,), (1,)), ((), ())), preferred_element_type=jnp.float32
    )
    for message in message_refs:
        unit = unit_of(as_float(message[2 * tokens :, :]))
        pre = pre + as_float(message[:tokens, :]) * unit[0:1]
        grad = grad + as_float(message[tokens : 2 * tokens, :]) * unit[1:2]
    return pre, grad


def send_kernel(tokens, n_messages, where_ref, rows_ref, enc_ref, dec_ref, *refs):
    messages, out_ref = refs[:n_messages], refs[-1]
    pre, grad = partial_sums(tokens, rows_ref, enc_ref, dec_ref, messages)
    pre_code = scale_code(jnp.max(jnp.abs(pre), axis=0, keepdims=True))
    grad_code = scale_code(jnp.max(jnp.abs(grad), axis=0, keepdims=True))
    out_ref[:tokens, :] = quantise(pre, pre_code)
    out_ref[tokens : 2 * tokens, :] = quantise(grad, grad_code)
    row = lax.broadcasted_iota(jnp.int32, (CODE_ROWS, pre.shape[1]), 0)
    codes = jnp.where(row == 0, pre_code, jnp.where(row == 1, grad_code, 0.0))
    out_ref[2 * tokens :, :] = codes.astype(jnp.int32).astype(jnp.int16)


def credit_kernel(tokens, n_messages, where_ref, rows_ref, enc_ref, dec_ref, *refs):
    messages = refs[:n_messages]
    bias_ref, routing_ref, out_ref, code_ref = refs[n_messages], refs[n_messages + 1], refs[-2], refs[-1]
    pre, grad = partial_sums(tokens, rows_ref, enc_ref, dec_ref, messages)
    score = jnp.maximum(pre + bias_ref[...], 0.0) * grad
    high = score.astype(jnp.bfloat16)
    low = (score - high.astype(jnp.float32)).astype(jnp.bfloat16)
    credit = jnp.dot(routing_ref[...], high, preferred_element_type=jnp.float32) + jnp.dot(
        routing_ref[...], low, preferred_element_type=jnp.float32
    )
    code = scale_code(jnp.max(jnp.abs(credit), axis=1, keepdims=True))
    out_ref[...] = quantise(credit, code)
    code_ref[...] = jnp.broadcast_to(code, (E, LANES)).astype(jnp.int32).astype(jnp.int16)


def block_of(length, most=512):
    block = min(length, most)
    while length % block:
        block -= LANES
    return block


class Chunk:
    def __init__(self, first, size, order):
        self.first, self.size, self.order = first, size, order
        self.messages = []

    def kept(self, bits, stage):
        first = self.first
        for j in range(stage):
            first = first + bits[self.order[j]] * (self.size >> (j + 1))
        return first

    def sent(self, bits, stage):
        return self.kept(bits, stage) + (1 - bits[self.order[stage]]) * (self.size >> (stage + 1))


def run_stage(chunk, stage, bits, rows, enc, dec, bias, routing, earlier, cost):
    last = stage == len(chunk.order)
    tokens, depth = rows.shape[1:]
    length = chunk.size >> (stage if last else stage + 1)
    block = block_of(length)

    def at(i, bits_ref, message=None):
        first = chunk.kept(bits_ref, stage) if last else chunk.sent(bits_ref, stage)
        if message is not None:
            first = first - chunk.kept(bits_ref, message + 1)
        return first // block + i

    in_specs = [
        pl.BlockSpec((2, tokens, depth), lambda i, w: (0, 0, 0)),
        pl.BlockSpec((depth, block), lambda i, w: (0, at(i, w))),
        pl.BlockSpec((block, depth), lambda i, w: (at(i, w), 0)),
    ]
    operands = [rows, enc, dec]
    for j, message in enumerate(chunk.messages):
        in_specs.append(pl.BlockSpec((message.shape[0], block), lambda i, w, j=j: (0, at(i, w, j))))
        operands.append(message)
    if last:
        in_specs.append(pl.BlockSpec((1, block), lambda i, w: (0, at(i, w))))
        in_specs.append(pl.BlockSpec(routing.shape, lambda i, w: (0, 0)))
        operands += [bias, routing]
        body = credit_kernel
        out_shape = [
            jax.ShapeDtypeStruct((E, length), jnp.int16),
            jax.ShapeDtypeStruct((E, LANES * (length // block)), jnp.int16),
        ]
        out_specs = [pl.BlockSpec((E, block), lambda i, w: (0, i)), pl.BlockSpec((E, LANES), lambda i, w: (0, i))]
    else:
        body = send_kernel
        out_shape = jax.ShapeDtypeStruct((2 * tokens + CODE_ROWS, length), jnp.int16)
        out_specs = pl.BlockSpec((2 * tokens + CODE_ROWS, block), lambda i, w: (0, i))
    if earlier is not None:
        in_specs.append(pl.BlockSpec(memory_space=pl.ANY))
        operands.append(earlier)
    return pl.pallas_call(
        functools.partial(body, tokens, len(chunk.messages)),
        grid_spec=pltpu.PrefetchScalarGridSpec(
            num_scalar_prefetch=1, grid=(length // block,), in_specs=in_specs, out_specs=out_specs
        ),
        out_shape=out_shape,
        compiler_params=pltpu.CompilerParams(vmem_limit_bytes=40 * 1024 * 1024),
        cost_estimate=pl.CostEstimate(flops=cost, bytes_accessed=1, transcendentals=0),
        name=("credit" if last else f"stage{stage}"),
    )(bits, *operands)


def place_kernel(blocks, whole_ref, *refs):
    out_ref = refs[-1]
    lanes = whole_ref.shape[2] - LANES
    for owner, column, width, lane, target in blocks:
        unit = unit_of(as_float(whole_ref[owner, :, lanes:])[:, lane : lane + 1])
        out_ref[:, target : target + width] = as_float(whole_ref[owner, :, column : column + width]) * unit


def place(group, n_dp, whole, out, features, earlier):
    first = min(chunk.first for chunk in group)
    span = sum(chunk.size for chunk in group)
    blocks, column = [], 0
    for lane, chunk in enumerate(group):
        width = chunk.size // n_dp
        for owner in range(n_dp):
            slot = 0
            for bit in chunk.order:
                slot = 2 * slot + ((owner >> bit) & 1)
            blocks.append((owner, column, width, lane, chunk.first - first + slot * width))
        column += width
    operands = [whole, earlier]
    in_specs = [pl.BlockSpec(whole.shape, lambda i: (0, 0, 0)), pl.BlockSpec(memory_space=pl.ANY)]
    if out is not None and out is not earlier:
        operands.append(out)
        in_specs.append(pl.BlockSpec(memory_space=pl.ANY))
    return pl.pallas_call(
        functools.partial(place_kernel, blocks),
        grid=(1,),
        in_specs=in_specs,
        out_specs=pl.BlockSpec((whole.shape[1], span), lambda i: (0, first // span)),
        out_shape=jax.ShapeDtypeStruct((whole.shape[1], features), jnp.float32),
        input_output_aliases={} if out is None else {len(operands) - 1: 0},
        compiler_params=pltpu.CompilerParams(vmem_limit_bytes=40 * 1024 * 1024),
        name="place",
    )(*operands)


def collect(credits, n_dp):
    lane = lax.broadcasted_iota(jnp.int32, (E, LANES), 1)
    codes = credits[0][1]
    for k in range(1, len(credits)):
        codes = jnp.where(lane == k, credits[k][1], codes)
    whole = jnp.concatenate([c[0] for c in credits] + [codes], 1)
    whole = lax.all_to_all(whole, "dp", split_axis=0, concat_axis=0, tiled=True)
    return whole.reshape(n_dp, E // n_dp, -1)


def plan_of(units, n_bits):
    straight = tuple(range(n_bits))
    if units == 16 and n_bits == 3:
        sizes = SIZES
        groups, sequence = GROUPS, SEQUENCE
    else:
        sizes = [(1, straight)] * units
        groups, sequence = [list(range(units))], None
    if sequence is None:
        sequence = [
            (step - stage, stage)
            for step in range(len(sizes) + n_bits)
            for stage in range(n_bits + 1)
            if 0 <= step - stage < len(sizes)
        ]
    return sizes, groups, sequence


A, B, C, D = (0, 1, 2), (1, 0, 2), (1, 2, 0), (0, 2, 1)
SIZES = [(4, A), (4, C), (4, A), (2, D), (2, A)]
GROUPS = [[0, 1, 2, 3, 4]]
SEQUENCE = [
    (0, 0), (1, 0), (2, 0), (0, 1), (1, 1), (3, 0), (2, 1), (0, 2), (4, 0), (1, 2),
    (3, 1), (4, 1), (2, 2), (0, 3), (1, 3), (3, 2), (4, 2), (2, 3), (3, 3), (4, 3),
]
COSTS = [9224000000]


def route_table(routes):
    experts, buckets = routes[:, : routes.shape[1] // 2], routes[:, routes.shape[1] // 2 :]
    expert_ids = jnp.arange(E, dtype=jnp.int32)
    weights = buckets.astype(jnp.float32) * 0.125
    table = jnp.sum(
        (experts[:, None, :].astype(jnp.int32) == expert_ids[None, :, None]).astype(jnp.float32)
        * weights[:, None, :],
        axis=2,
    )
    return table.T.astype(jnp.bfloat16)


def gather_rows(residual, cotangent, route_experts, route_buckets, n_dp):
    mine, width = residual.shape
    depth = width // n_dp
    n_feat, core = lax.axis_size("feat"), lax.axis_index("feat") & 1
    routes = jnp.concatenate([route_experts, route_buckets], 1).astype(jnp.bfloat16)
    n_route = routes.shape[1]
    extra = jnp.broadcast_to(jnp.pad(routes, ((0, 0), (0, LANES - n_route)))[:, None, :], (mine, n_dp, LANES))
    own = jnp.where(core == 0, residual, cotangent).reshape(mine, n_dp, depth)
    own = jnp.concatenate([own, extra], 2).transpose(1, 0, 2)
    got = lax.all_to_all(own, "dp", split_axis=0, concat_axis=0, tiled=True)
    got = got.reshape(n_dp * mine, depth + LANES)
    first, routes = got[:, :depth], got[:, depth : depth + n_route]
    second = lax.ppermute(first, "feat", [(i, i ^ 1) for i in range(n_feat)])
    rows = jnp.where(core == 0, jnp.stack([first, second]), jnp.stack([second, first]))
    return rows, routes


def on_device(residual, cotangent, enc, bias, dec, route_experts, route_buckets):
    n_dp, me = lax.axis_size("dp"), lax.axis_index("dp")
    n_bits = n_dp.bit_length() - 1
    features = enc.shape[1]
    bits = (me >> jnp.arange(n_bits, dtype=jnp.int32)) & 1
    rows, routes = gather_rows(residual, cotangent, route_experts, route_buckets, n_dp)
    routing = route_table(routes)
    bias = bias[None, :]

    unit = LANES * n_dp
    sizes, groups, sequence = plan_of(features // unit, n_bits)
    chunks, first = [], 0
    for units, order in sizes:
        chunks.append(Chunk(first, units * unit, order))
        first += units * unit

    earlier, credits, sent, out = None, {}, {}, None
    for n, (c, stage) in enumerate(sequence + [(-1, g) for g in range(len(groups)) if (-1, g) not in sequence]):
        if c < 0:
            group = [chunks[k] for k in groups[stage]]
            out = earlier = place(group, n_dp, sent[stage], out, features, earlier)
            continue
        chunk = chunks[c]
        result = run_stage(chunk, stage, bits, rows, enc, dec, bias, routing, earlier, COSTS[min(n, len(COSTS) - 1)])
        if stage < n_bits:
            partner = [(i, i ^ (1 << chunk.order[stage])) for i in range(n_dp)]
            chunk.messages.append(lax.ppermute(result, "dp", partner))
            earlier = result
        else:
            credits[c] = result
            earlier = result[1]
            for g, group in enumerate(groups):
                if c in group and all(k in credits for k in group):
                    sent[g] = collect([credits[k] for k in group], n_dp)
    return out


def solution(mesh):
    placed = (
        P("dp", None),
        P("dp", None),
        P("dp", "feat"),
        P("feat"),
        P("feat", "dp"),
        P("dp", None),
        P("dp", None),
    )
    return jax.shard_map(
        on_device, mesh=mesh, in_specs=placed, out_specs=P("dp", "feat"), check_vma=False
    )
```

```python
import functools

import jax
import jax.numpy as jnp
from jax import lax
from jax.experimental import pallas as pl
from jax.experimental.pallas import tpu as pltpu
from jax.sharding import PartitionSpec as P

E = 256
LANES = 128
CODE_ROWS = 8
STEPS = 256.0
TOP = 32700.0
TINY = 2.0 ** -100


def scale_code(most):
    return jnp.ceil(jnp.log2(jnp.maximum(most, TINY)) * STEPS)


def quantise(value, code):
    return jnp.round(value * (jnp.exp2(code * (-1.0 / STEPS)) * TOP)).astype(jnp.int32).astype(jnp.int16)


def unit_of(code):
    return jnp.exp2(code * (1.0 / STEPS)) * (1.0 / TOP)


def as_float(ints):
    return ints.astype(jnp.int32).astype(jnp.float32)


def partial_sums(tokens, rows_ref, enc_ref, dec_ref, message_refs):
    pre = jnp.dot(rows_ref[0], enc_ref[...], preferred_element_type=jnp.float32)
    grad = lax.dot_general(
        rows_ref[1], dec_ref[...], (((1,), (1,)), ((), ())), preferred_element_type=jnp.float32
    )
    for message in message_refs:
        unit = unit_of(as_float(message[2 * tokens :, :]))
        pre = pre + as_float(message[:tokens, :]) * unit[0:1]
        grad = grad + as_float(message[tokens : 2 * tokens, :]) * unit[1:2]
    return pre, grad


def send_kernel(tokens, n_messages, where_ref, rows_ref, enc_ref, dec_ref, *refs):
    messages, out_ref = refs[:n_messages], refs[-1]
    pre, grad = partial_sums(tokens, rows_ref, enc_ref, dec_ref, messages)
    pre_code = scale_code(jnp.max(jnp.abs(pre), axis=0, keepdims=True))
    grad_code = scale_code(jnp.max(jnp.abs(grad), axis=0, keepdims=True))
    out_ref[:tokens, :] = quantise(pre, pre_code)
    out_ref[tokens : 2 * tokens, :] = quantise(grad, grad_code)
    row = lax.broadcasted_iota(jnp.int32, (CODE_ROWS, pre.shape[1]), 0)
    codes = jnp.where(row == 0, pre_code, jnp.where(row == 1, grad_code, 0.0))
    out_ref[2 * tokens :, :] = codes.astype(jnp.int32).astype(jnp.int16)


def credit_kernel(tokens, n_messages, where_ref, rows_ref, enc_ref, dec_ref, *refs):
    messages = refs[:n_messages]
    bias_ref, routing_ref, out_ref, code_ref = refs[n_messages], refs[n_messages + 1], refs[-2], refs[-1]
    pre, grad = partial_sums(tokens, rows_ref, enc_ref, dec_ref, messages)
    score = jnp.maximum(pre + bias_ref[...], 0.0) * grad
    high = score.astype(jnp.bfloat16)
    low = (score - high.astype(jnp.float32)).astype(jnp.bfloat16)
    credit = jnp.dot(routing_ref[...], high, preferred_element_type=jnp.float32) + jnp.dot(
        routing_ref[...], low, preferred_element_type=jnp.float32
    )
    code = scale_code(jnp.max(jnp.abs(credit), axis=1, keepdims=True))
    out_ref[...] = quantise(credit, code)
    code_ref[...] = jnp.broadcast_to(code, (E, LANES)).astype(jnp.int32).astype(jnp.int16)


def block_of(length, most=512):
    block = min(length, most)
    while length % block:
        block -= LANES
    return block


class Chunk:
    def __init__(self, first, size, order):
        self.first, self.size, self.order = first, size, order
        self.messages = []

    def kept(self, bits, stage):
        first = self.first
        for j in range(stage):
            first = first + bits[self.order[j]] * (self.size >> (j + 1))
        return first

    def sent(self, bits, stage):
        return self.kept(bits, stage) + (1 - bits[self.order[stage]]) * (self.size >> (stage + 1))


def run_stage(chunk, stage, bits, rows, enc, dec, bias, routing, earlier, cost):
    last = stage == len(chunk.order)
    tokens, depth = rows.shape[1:]
    length = chunk.size >> (stage if last else stage + 1)
    block = block_of(length)

    def at(i, bits_ref, message=None):
        first = chunk.kept(bits_ref, stage) if last else chunk.sent(bits_ref, stage)
        if message is not None:
            first = first - chunk.kept(bits_ref, message + 1)
        return first // block + i

    in_specs = [
        pl.BlockSpec(memory_space=pltpu.VMEM),
        pl.BlockSpec((depth, block), lambda i, w: (0, at(i, w))),
        pl.BlockSpec((block, depth), lambda i, w: (at(i, w), 0)),
    ]
    operands = [rows, enc, dec]
    for j, message in enumerate(chunk.messages):
        in_specs.append(pl.BlockSpec((message.shape[0], block), lambda i, w, j=j: (0, at(i, w, j))))
        operands.append(message)
    if last:
        in_specs.append(pl.BlockSpec((1, block), lambda i, w: (0, at(i, w))))
        in_specs.append(pl.BlockSpec(memory_space=pltpu.VMEM))
        operands += [bias, routing]
        body = credit_kernel
        out_shape = [
            jax.ShapeDtypeStruct((E, length), jnp.int16),
            jax.ShapeDtypeStruct((E, LANES * (length // block)), jnp.int16),
        ]
        out_specs = [pl.BlockSpec((E, block), lambda i, w: (0, i)), pl.BlockSpec((E, LANES), lambda i, w: (0, i))]
    else:
        body = send_kernel
        out_shape = jax.ShapeDtypeStruct((2 * tokens + CODE_ROWS, length), jnp.int16)
        out_specs = pl.BlockSpec((2 * tokens + CODE_ROWS, block), lambda i, w: (0, i))
    if earlier is not None:
        in_specs.append(pl.BlockSpec(memory_space=pl.ANY))
        operands.append(earlier)
    return pl.pallas_call(
        functools.partial(body, tokens, len(chunk.messages)),
        grid_spec=pltpu.PrefetchScalarGridSpec(
            num_scalar_prefetch=1, grid=(length // block,), in_specs=in_specs, out_specs=out_specs
        ),
        out_shape=out_shape,
        compiler_params=pltpu.CompilerParams(vmem_limit_bytes=40 * 1024 * 1024),
        cost_estimate=pl.CostEstimate(flops=cost, bytes_accessed=1, transcendentals=0),
        name=("credit" if last else f"stage{stage}"),
    )(bits, *operands)


def place_kernel(blocks, whole_ref, *refs):
    out_ref = refs[-1]
    lanes = whole_ref.shape[2] - LANES
    for owner, column, width, lane, target in blocks:
        unit = unit_of(as_float(whole_ref[owner, :, lanes:])[:, lane : lane + 1])
        out_ref[:, target : target + width] = as_float(whole_ref[owner, :, column : column + width]) * unit


def place(group, n_dp, whole, out, features, earlier):
    first = min(chunk.first for chunk in group)
    span = sum(chunk.size for chunk in group)
    blocks, column = [], 0
    for lane, chunk in enumerate(group):
        width = chunk.size // n_dp
        for owner in range(n_dp):
            slot = 0
            for bit in chunk.order:
                slot = 2 * slot + ((owner >> bit) & 1)
            blocks.append((owner, column, width, lane, chunk.first - first + slot * width))
        column += width
    operands = [whole, earlier]
    in_specs = [pl.BlockSpec(whole.shape, lambda i: (0, 0, 0)), pl.BlockSpec(memory_space=pl.ANY)]
    if out is not None and out is not earlier:
        operands.append(out)
        in_specs.append(pl.BlockSpec(memory_space=pl.ANY))
    return pl.pallas_call(
        functools.partial(place_kernel, blocks),
        grid=(1,),
        in_specs=in_specs,
        out_specs=pl.BlockSpec((whole.shape[1], span), lambda i: (0, first // span)),
        out_shape=jax.ShapeDtypeStruct((whole.shape[1], features), jnp.float32),
        input_output_aliases={} if out is None else {len(operands) - 1: 0},
        compiler_params=pltpu.CompilerParams(vmem_limit_bytes=40 * 1024 * 1024),
        name="place",
    )(*operands)


def collect(credits, n_dp):
    lane = lax.broadcasted_iota(jnp.int32, (E, LANES), 1)
    codes = credits[0][1]
    for k in range(1, len(credits)):
        codes = jnp.where(lane == k, credits[k][1], codes)
    whole = jnp.concatenate([c[0] for c in credits] + [codes], 1)
    whole = lax.all_to_all(whole, "dp", split_axis=0, concat_axis=0, tiled=True)
    return whole.reshape(n_dp, E // n_dp, -1)


def plan_of(units, n_bits):
    straight = tuple(range(n_bits))
    if units == 16 and n_bits == 3:
        sizes = SIZES
        groups, sequence = GROUPS, SEQUENCE
    else:
        sizes = [(1, straight)] * units
        groups, sequence = [list(range(units))], None
    if sequence is None:
        sequence = [
            (step - stage, stage)
            for step in range(len(sizes) + n_bits)
            for stage in range(n_bits + 1)
            if 0 <= step - stage < len(sizes)
        ]
    return sizes, groups, sequence


A, B, C, D = (0, 1, 2), (1, 0, 2), (1, 2, 0), (0, 2, 1)
SIZES = [(2, A), (2, C), (2, A), (2, A), (2, B), (2, A), (2, A), (1, D), (1, A)]
GROUPS = [[0, 1, 2, 3], [4, 5, 6, 7, 8]]
SEQUENCE = [
    (0, 0), (1, 0), (2, 0), (3, 0), (0, 1), (1, 1), (4, 0), (0, 2), (2, 1), (1, 2),
    (5, 0), (3, 1), (1, 3), (0, 3), (4, 1), (6, 0), (2, 2), (5, 1), (3, 2), (4, 2),
    (7, 0), (2, 3), (3, 3), (8, 0), (6, 1), (5, 2), (7, 1), (4, 3), (8, 1), (-1, 0),
    (6, 2), (7, 2), (8, 2), (5, 3), (7, 3), (6, 3), (8, 3),
]
COSTS = [2306000000]


def route_table(routes):
    experts, buckets = routes[:, : routes.shape[1] // 2], routes[:, routes.shape[1] // 2 :]
    expert_ids = jnp.arange(E, dtype=jnp.int32)
    weights = buckets.astype(jnp.float32) * 0.125
    table = jnp.sum(
        (experts[:, None, :].astype(jnp.int32) == expert_ids[None, :, None]).astype(jnp.float32)
        * weights[:, None, :],
        axis=2,
    )
    return table.T.astype(jnp.bfloat16)


def gather_rows(residual, cotangent, route_experts, route_buckets, n_dp):
    mine, width = residual.shape
    depth = width // n_dp
    n_feat, core = lax.axis_size("feat"), lax.axis_index("feat") & 1
    routes = jnp.concatenate([route_experts, route_buckets], 1).astype(jnp.bfloat16)
    n_route = routes.shape[1]
    extra = jnp.broadcast_to(jnp.pad(routes, ((0, 0), (0, LANES - n_route)))[:, None, :], (mine, n_dp, LANES))
    own = jnp.where(core == 0, residual, cotangent).reshape(mine, n_dp, depth)
    own = jnp.concatenate([own, extra], 2).transpose(1, 0, 2)
    got = lax.all_to_all(own, "dp", split_axis=0, concat_axis=0, tiled=True)
    got = got.reshape(n_dp * mine, depth + LANES)
    first, routes = got[:, :depth], got[:, depth : depth + n_route]
    second = lax.ppermute(first, "feat", [(i, i ^ 1) for i in range(n_feat)])
    rows = jnp.where(core == 0, jnp.stack([first, second]), jnp.stack([second, first]))
    return rows, routes


def on_device(residual, cotangent, enc, bias, dec, route_experts, route_buckets):
    n_dp, me = lax.axis_size("dp"), lax.axis_index("dp")
    n_bits = n_dp.bit_length() - 1
    features = enc.shape[1]
    bits = (me >> jnp.arange(n_bits, dtype=jnp.int32)) & 1
    rows, routes = gather_rows(residual, cotangent, route_experts, route_buckets, n_dp)
    routing = route_table(routes)
    bias = bias[None, :]

    unit = LANES * n_dp
    sizes, groups, sequence = plan_of(features // unit, n_bits)
    chunks, first = [], 0
    for units, order in sizes:
        chunks.append(Chunk(first, units * unit, order))
        first += units * unit

    earlier, credits, sent, out = None, {}, {}, None
    for n, (c, stage) in enumerate(sequence + [(-1, g) for g in range(len(groups)) if (-1, g) not in sequence]):
        if c < 0:
            group = [chunks[k] for k in groups[stage]]
            out = earlier = place(group, n_dp, sent[stage], out, features, earlier)
            continue
        chunk = chunks[c]
        result = run_stage(chunk, stage, bits, rows, enc, dec, bias, routing, earlier, COSTS[min(n, len(COSTS) - 1)])
        if stage < n_bits:
            partner = [(i, i ^ (1 << chunk.order[stage])) for i in range(n_dp)]
            chunk.messages.append(lax.ppermute(result, "dp", partner))
            earlier = result
        else:
            credits[c] = result
            earlier = result[1]
            for g, group in enumerate(groups):
                if c in group and all(k in credits for k in group):
                    sent[g] = collect([credits[k] for k in group], n_dp)
    return out


def solution(mesh):
    placed = (
        P("dp", None),
        P("dp", None),
        P("dp", "feat"),
        P("feat"),
        P("feat", "dp"),
        P("dp", None),
        P("dp", None),
    )
    return jax.shard_map(
        on_device, mesh=mesh, in_specs=placed, out_specs=P("dp", "feat"), check_vma=False
    )
```

```python
import functools

import jax
import jax.numpy as jnp
from jax import lax
from jax.experimental import pallas as pl
from jax.experimental.pallas import tpu as pltpu
from jax.sharding import PartitionSpec as P

E = 256
LANES = 128
CODE_ROWS = 8
STEPS = 256.0
TOP = 32700.0
TINY = 2.0 ** -100


def scale_code(most):
    return jnp.ceil(jnp.log2(jnp.maximum(most, TINY)) * STEPS)


def quantise(value, code):
    return jnp.round(value * (jnp.exp2(code * (-1.0 / STEPS)) * TOP)).astype(jnp.int32).astype(jnp.int16)


def unit_of(code):
    return jnp.exp2(code * (1.0 / STEPS)) * (1.0 / TOP)


def as_float(ints):
    return ints.astype(jnp.int32).astype(jnp.float32)


def partial_sums(tokens, rows_ref, enc_ref, dec_ref, message_refs):
    pre = jnp.dot(rows_ref[0], enc_ref[...], preferred_element_type=jnp.float32)
    grad = lax.dot_general(
        rows_ref[1], dec_ref[...], (((1,), (1,)), ((), ())), preferred_element_type=jnp.float32
    )
    for message in message_refs:
        unit = unit_of(as_float(message[2 * tokens :, :]))
        pre = pre + as_float(message[:tokens, :]) * unit[0:1]
        grad = grad + as_float(message[tokens : 2 * tokens, :]) * unit[1:2]
    return pre, grad


def send_kernel(tokens, n_messages, where_ref, rows_ref, enc_ref, dec_ref, *refs):
    messages, out_ref = refs[:n_messages], refs[-1]
    pre, grad = partial_sums(tokens, rows_ref, enc_ref, dec_ref, messages)
    pre_code = scale_code(jnp.max(jnp.abs(pre), axis=0, keepdims=True))
    grad_code = scale_code(jnp.max(jnp.abs(grad), axis=0, keepdims=True))
    out_ref[:tokens, :] = quantise(pre, pre_code)
    out_ref[tokens : 2 * tokens, :] = quantise(grad, grad_code)
    row = lax.broadcasted_iota(jnp.int32, (CODE_ROWS, pre.shape[1]), 0)
    codes = jnp.where(row == 0, pre_code, jnp.where(row == 1, grad_code, 0.0))
    out_ref[2 * tokens :, :] = codes.astype(jnp.int32).astype(jnp.int16)


def credit_kernel(tokens, n_messages, where_ref, rows_ref, enc_ref, dec_ref, *refs):
    messages = refs[:n_messages]
    bias_ref, routing_ref, out_ref, code_ref = refs[n_messages], refs[n_messages + 1], refs[-2], refs[-1]
    pre, grad = partial_sums(tokens, rows_ref, enc_ref, dec_ref, messages)
    score = jnp.maximum(pre + bias_ref[...], 0.0) * grad
    high = score.astype(jnp.bfloat16)
    low = (score - high.astype(jnp.float32)).astype(jnp.bfloat16)
    credit = jnp.dot(routing_ref[...], high, preferred_element_type=jnp.float32) + jnp.dot(
        routing_ref[...], low, preferred_element_type=jnp.float32
    )
    code = scale_code(jnp.max(jnp.abs(credit), axis=1, keepdims=True))
    out_ref[...] = quantise(credit, code)
    code_ref[...] = jnp.broadcast_to(code, (E, LANES)).astype(jnp.int32).astype(jnp.int16)


def block_of(length, most=512):
    block = min(length, most)
    while length % block:
        block -= LANES
    return block


class Chunk:
    def __init__(self, first, size, order):
        self.first, self.size, self.order = first, size, order
        self.messages = []

    def kept(self, bits, stage):
        first = self.first
        for j in range(stage):
            first = first + bits[self.order[j]] * (self.size >> (j + 1))
        return first

    def sent(self, bits, stage):
        return self.kept(bits, stage) + (1 - bits[self.order[stage]]) * (self.size >> (stage + 1))


def run_stage(chunk, stage, bits, rows, enc, dec, bias, routing, earlier, cost):
    last = stage == len(chunk.order)
    tokens, depth = rows.shape[1:]
    length = chunk.size >> (stage if last else stage + 1)
    block = block_of(length)

    def at(i, bits_ref, message=None):
        first = chunk.kept(bits_ref, stage) if last else chunk.sent(bits_ref, stage)
        if message is not None:
            first = first - chunk.kept(bits_ref, message + 1)
        return first // block + i

    in_specs = [
        pl.BlockSpec(memory_space=pltpu.VMEM),
        pl.BlockSpec((depth, block), lambda i, w: (0, at(i, w))),
        pl.BlockSpec((block, depth), lambda i, w: (at(i, w), 0)),
    ]
    operands = [rows, enc, dec]
    for j, message in enumerate(chunk.messages):
        in_specs.append(pl.BlockSpec((message.shape[0], block), lambda i, w, j=j: (0, at(i, w, j))))
        operands.append(message)
    if last:
        in_specs.append(pl.BlockSpec((1, block), lambda i, w: (0, at(i, w))))
        in_specs.append(pl.BlockSpec(memory_space=pltpu.VMEM))
        operands += [bias, routing]
        body = credit_kernel
        out_shape = [
            jax.ShapeDtypeStruct((E, length), jnp.int16),
            jax.ShapeDtypeStruct((E, LANES * (length // block)), jnp.int16),
        ]
        out_specs = [pl.BlockSpec((E, block), lambda i, w: (0, i)), pl.BlockSpec((E, LANES), lambda i, w: (0, i))]
    else:
        body = send_kernel
        out_shape = jax.ShapeDtypeStruct((2 * tokens + CODE_ROWS, length), jnp.int16)
        out_specs = pl.BlockSpec((2 * tokens + CODE_ROWS, block), lambda i, w: (0, i))
    if earlier is not None:
        in_specs.append(pl.BlockSpec(memory_space=pl.ANY))
        operands.append(earlier)
    return pl.pallas_call(
        functools.partial(body, tokens, len(chunk.messages)),
        grid_spec=pltpu.PrefetchScalarGridSpec(
            num_scalar_prefetch=1, grid=(length // block,), in_specs=in_specs, out_specs=out_specs
        ),
        out_shape=out_shape,
        compiler_params=pltpu.CompilerParams(vmem_limit_bytes=40 * 1024 * 1024),
        cost_estimate=pl.CostEstimate(flops=cost, bytes_accessed=1, transcendentals=0),
        name=("credit" if last else f"stage{stage}"),
    )(bits, *operands)


def place_kernel(blocks, whole_ref, *refs):
    out_ref = refs[-1]
    lanes = whole_ref.shape[2] - LANES
    for owner, column, width, lane, target in blocks:
        unit = unit_of(as_float(whole_ref[owner, :, lanes:])[:, lane : lane + 1])
        out_ref[:, target : target + width] = as_float(whole_ref[owner, :, column : column + width]) * unit


def place(group, n_dp, whole, out, features, earlier):
    first = min(chunk.first for chunk in group)
    span = sum(chunk.size for chunk in group)
    blocks, column = [], 0
    for lane, chunk in enumerate(group):
        width = chunk.size // n_dp
        for owner in range(n_dp):
            slot = 0
            for bit in chunk.order:
                slot = 2 * slot + ((owner >> bit) & 1)
            blocks.append((owner, column, width, lane, chunk.first - first + slot * width))
        column += width
    operands = [whole, earlier]
    in_specs = [pl.BlockSpec(whole.shape, lambda i: (0, 0, 0)), pl.BlockSpec(memory_space=pl.ANY)]
    if out is not None and out is not earlier:
        operands.append(out)
        in_specs.append(pl.BlockSpec(memory_space=pl.ANY))
    return pl.pallas_call(
        functools.partial(place_kernel, blocks),
        grid=(1,),
        in_specs=in_specs,
        out_specs=pl.BlockSpec((whole.shape[1], span), lambda i: (0, first // span)),
        out_shape=jax.ShapeDtypeStruct((whole.shape[1], features), jnp.float32),
        input_output_aliases={} if out is None else {len(operands) - 1: 0},
        compiler_params=pltpu.CompilerParams(vmem_limit_bytes=40 * 1024 * 1024),
        name="place",
    )(*operands)


def collect(credits, n_dp):
    lane = lax.broadcasted_iota(jnp.int32, (E, LANES), 1)
    codes = credits[0][1]
    for k in range(1, len(credits)):
        codes = jnp.where(lane == k, credits[k][1], codes)
    whole = jnp.concatenate([c[0] for c in credits] + [codes], 1)
    whole = lax.all_to_all(whole, "dp", split_axis=0, concat_axis=0, tiled=True)
    return whole.reshape(n_dp, E // n_dp, -1)


def plan_of(units, n_bits):
    straight = tuple(range(n_bits))
    if units == 16 and n_bits == 3:
        sizes = SIZES
        groups, sequence = GROUPS, SEQUENCE
    else:
        sizes = [(1, straight)] * units
        groups, sequence = [list(range(units))], None
    if sequence is None:
        sequence = [
            (step - stage, stage)
            for step in range(len(sizes) + n_bits)
            for stage in range(n_bits + 1)
            if 0 <= step - stage < len(sizes)
        ]
    return sizes, groups, sequence


A, B, C, D = (0, 1, 2), (1, 0, 2), (1, 2, 0), (0, 2, 1)
SIZES = [(2, A), (2, C), (2, A), (2, A), (2, B), (2, A), (2, A), (1, D), (1, A)]
GROUPS = [[0, 1, 2, 3], [4, 5, 6, 7, 8]]
SEQUENCE = [
    (0, 0), (1, 0), (2, 0), (3, 0), (0, 1), (1, 1), (4, 0), (0, 2), (2, 1), (1, 2),
    (5, 0), (3, 1), (1, 3), (0, 3), (4, 1), (6, 0), (2, 2), (5, 1), (3, 2), (4, 2),
    (7, 0), (2, 3), (3, 3), (8, 0), (6, 1), (5, 2), (7, 1), (4, 3), (8, 1), (-1, 0),
    (6, 2), (7, 2), (8, 2), (5, 3), (7, 3), (6, 3), (8, 3),
]
COSTS = [2306000000] * 31 + [576500000] * 6


def route_table(routes):
    experts, buckets = routes[:, : routes.shape[1] // 2], routes[:, routes.shape[1] // 2 :]
    expert_ids = jnp.arange(E, dtype=jnp.int32)
    weights = buckets.astype(jnp.float32) * 0.125
    table = jnp.sum(
        (experts[:, None, :].astype(jnp.int32) == expert_ids[None, :, None]).astype(jnp.float32)
        * weights[:, None, :],
        axis=2,
    )
    return table.T.astype(jnp.bfloat16)


def gather_rows(residual, cotangent, route_experts, route_buckets, n_dp):
    mine, width = residual.shape
    depth = width // n_dp
    n_feat, core = lax.axis_size("feat"), lax.axis_index("feat") & 1
    routes = jnp.concatenate([route_experts, route_buckets], 1).astype(jnp.bfloat16)
    n_route = routes.shape[1]
    extra = jnp.broadcast_to(jnp.pad(routes, ((0, 0), (0, LANES - n_route)))[:, None, :], (mine, n_dp, LANES))
    own = jnp.where(core == 0, residual, cotangent).reshape(mine, n_dp, depth)
    own = jnp.concatenate([own, extra], 2).transpose(1, 0, 2)
    got = lax.all_to_all(own, "dp", split_axis=0, concat_axis=0, tiled=True)
    got = got.reshape(n_dp * mine, depth + LANES)
    first, routes = got[:, :depth], got[:, depth : depth + n_route]
    second = lax.ppermute(first, "feat", [(i, i ^ 1) for i in range(n_feat)])
    rows = jnp.where(core == 0, jnp.stack([first, second]), jnp.stack([second, first]))
    return rows, routes


def on_device(residual, cotangent, enc, bias, dec, route_experts, route_buckets):
    n_dp, me = lax.axis_size("dp"), lax.axis_index("dp")
    n_bits = n_dp.bit_length() - 1
    features = enc.shape[1]
    bits = (me >> jnp.arange(n_bits, dtype=jnp.int32)) & 1
    rows, routes = gather_rows(residual, cotangent, route_experts, route_buckets, n_dp)
    routing = route_table(routes)
    bias = bias[None, :]

    unit = LANES * n_dp
    sizes, groups, sequence = plan_of(features // unit, n_bits)
    chunks, first = [], 0
    for units, order in sizes:
        chunks.append(Chunk(first, units * unit, order))
        first += units * unit

    earlier, credits, sent, out = None, {}, {}, None
    for n, (c, stage) in enumerate(sequence + [(-1, g) for g in range(len(groups)) if (-1, g) not in sequence]):
        if c < 0:
            group = [chunks[k] for k in groups[stage]]
            out = earlier = place(group, n_dp, sent[stage], out, features, earlier)
            continue
        chunk = chunks[c]
        result = run_stage(chunk, stage, bits, rows, enc, dec, bias, routing, earlier, COSTS[min(n, len(COSTS) - 1)])
        if stage < n_bits:
            partner = [(i, i ^ (1 << chunk.order[stage])) for i in range(n_dp)]
            chunk.messages.append(lax.ppermute(result, "dp", partner))
            earlier = result
        else:
            credits[c] = result
            earlier = result[1]
            for g, group in enumerate(groups):
                if c in group and all(k in credits for k in group):
                    sent[g] = collect([credits[k] for k in group], n_dp)
    return out


def solution(mesh):
    placed = (
        P("dp", None),
        P("dp", None),
        P("dp", "feat"),
        P("feat"),
        P("feat", "dp"),
        P("dp", None),
        P("dp", None),
    )
    return jax.shard_map(
        on_device, mesh=mesh, in_specs=placed, out_specs=P("dp", "feat"), check_vma=False
    )
```
